32 devices in a mesh: sk: 8 (over y, x, core), lang: 4 (over z).
Axes of the slice: x: 2, y: 2, z: 4, core: 2. Of those that a mesh axis runs over, the one named last changes fastest.
Arguments:
- embeddings: bfloat16 [32768, 1024], P(('sk', 'lang')), may hold values from -40 to 40
- omega: bfloat16 [32768, 256], P(('sk', 'lang')), may hold values from -0.03125 to 0.03125
- lang_ids: int32 [32768, 1], P(('sk', 'lang')), may hold values from 0 to 11; in each aligned block of 1024 rows (0 to 1023, 1024 to 2047, ...) at most 128 rows name the same one
Outputs:
- grouped: bfloat16 [49152, 256], P(('sk', 'lang'))
The draws below stay inside these ranges and needn't reach their ends.
Inputs may be any that keep to these rules, and one draw needn't show every extreme that they name: `lang_ids`: among the 1024 sentences of one device no language appears more than 128 times, and some language appears exactly 128 times.
All inputs are finite; a program needn't handle non-finite values.
Results may differ from the reference program's by a relative error of at most 0.0075.
Values may be sent and summed in bfloat16 or wider, within the bound.
A program may use at most 64 MiB of HBM per device.

```python
import math
import jax
import jax.numpy as jnp
import numpy as np
from jax import lax

D = 1024
SKETCH = 256
LANGS = 12
R_DEV = 1024
CAP = 128
ROWS = 32768
N_SK = 8
N_LANG = 4


def draw_embeddings(key, part):
    first_key, second_key = jax.random.split(key, 2)
    fourth_key = jax.random.fold_in(key, 17)
    fifth_key = jax.random.fold_in(key, 23)
    column_scale = jnp.exp(jax.random.uniform(second_key, (D,), jnp.float32, -1.2, 1.2))
    groups = ROWS // R_DEV
    directions = jnp.clip(jax.random.normal(fourth_key, (groups, D), jnp.float32), -4.0, 4.0)
    direction_rows = jnp.repeat(directions, R_DEV, axis=0)
    values = jnp.clip(jax.random.normal(first_key, (ROWS, D), jnp.float32), -5.0, 5.0)
    weights = jnp.clip(jax.random.normal(fifth_key, (ROWS, 1), jnp.float32), -3.0, 3.0)
    mixed = (values + weights * direction_rows) * column_scale[None, :]
    return jnp.clip(mixed, -40.0, 40.0).astype(jnp.bfloat16)


def level_of(rng, extent, cuts, low, top_value):
    def one(dim, parts):
        draws = jax.random.uniform(jax.random.fold_in(jax.random.fold_in(rng, 6), dim), (parts,), jnp.float32, low / len(cuts), top_value / len(cuts))
        return jnp.repeat(jnp.exp(draws), extent[dim] // parts).reshape((-1,) + (1,) * (len(extent) - dim - 1))

    gain = one(*cuts[0])
    for cut in cuts[1:]:
        gain = gain * one(*cut)
    return gain


def assign_block(rng, own, number, rows, count, top, most, slope):
    ranking = jax.random.permutation(rng, count)
    crowded, ordinary = shares(count, rows * top, most, slope, True), shares(count, rows * top, most, slope, False)
    places = jnp.arange(count)

    def named(tallies, offset_by):
        used = int((tallies > 0).sum())
        fixed = max(1, used // 4)
        passed = fixed + (places - fixed + offset_by * (used - fixed)) % max(1, count - fixed)
        return jnp.zeros((count,), jnp.int32).at[ranking[jnp.where(places < fixed, places, passed)]].set(jnp.asarray(tallies, jnp.int32))

    tallies = jnp.where(number % 4 == 0, named(crowded, number // 4), named(ordinary, number - number // 4 - 1))
    mixed = jax.random.permutation(jax.random.fold_in(own, 3), count)
    source_of, receiver = mixed[0:count // 2 * 2:2], mixed[1:count // 2 * 2:2]
    margin = jnp.minimum(tallies[source_of] - 1, most - tallies[receiver]) // 2
    margin = jnp.where((source_of == ranking[0]) | (receiver == ranking[0]) | (tallies[receiver] == 0), 0, jnp.maximum(margin, 0))
    passed = jax.random.randint(jax.random.fold_in(own, 4), (count // 2,), 0, 1 << 20) % (margin + 1)
    tallies = tallies.at[source_of].add(-passed).at[receiver].add(passed)
    labels = jnp.searchsorted(jnp.cumsum(tallies), jnp.arange(rows * top), side="right").astype(jnp.int32)
    grid = labels.reshape(top, rows).T
    grid = grid[jax.random.permutation(jax.random.fold_in(own, 1), rows)]
    offset_by = jax.random.randint(jax.random.fold_in(own, 2), (rows, 1), 0, top)
    return jnp.take_along_axis(grid, (jnp.arange(top)[None, :] + offset_by) % top, axis=1)


def shares(amount, total, reach, lean, full):
    portions = [(1 << 20) // math.isqrt(rank ** lean) + 1 for rank in range(1, amount + 1)]
    largest = reach if full else min(reach, max(-(-total // amount), total * portions[0] // sum(portions)))
    least = 1 if total - largest >= amount - 1 else 0
    holding, surplus = [largest] + [least] * (amount - 1), total - largest - least * (amount - 1)
    while surplus > 0:
        movable = [i for i in range(1, amount) if holding[i] < largest] or [i for i in range(1, amount) if holding[i] < reach]
        mass, left = sum([portions[i] for i in movable]), surplus
        for i in movable:
            addition = min(reach - holding[i], max(1, left * portions[i] // mass), surplus)
            holding[i] = holding[i] + addition
            surplus = surplus - addition
    return np.array(holding)


def normal_values(rng, shape, scale, most, pieces=(), kind=jnp.bfloat16):
    factor_of = level_of(rng, shape, pieces, -0.22, 0.18) if pieces else 1.0
    values = jax.random.normal(rng, shape, jnp.float32) * scale * factor_of
    return jnp.minimum(jnp.maximum(values, -most), most).astype(kind)


def setup_inputs(seed: int = 0) -> dict:
    streams_of = jax.random.split(jax.random.key(seed), 4)
    embeddings = draw_embeddings(jax.random.fold_in(streams_of[3], 71), 0)
    omega = normal_values(streams_of[1], (ROWS, SKETCH), ROWS ** -0.5, 0.03125, ((0, 32),))
    lang_ids_keys = jax.random.split(jax.random.fold_in(streams_of[2], 1), ROWS // R_DEV)
    lang_ids_turns = jax.random.permutation(jax.random.fold_in(streams_of[2], 3), ROWS // R_DEV)
    lang_ids = jax.vmap(lambda own, number: assign_block(jax.random.fold_in(streams_of[2], 2), own, number, R_DEV, LANGS, 1, CAP, 2))(lang_ids_keys, lang_ids_turns).reshape((ROWS, 1))
    return {"embeddings": embeddings, "omega": omega, "lang_ids": lang_ids}


def orthonormal(sketch):
    gram_matrix = jnp.dot(sketch.astype(jnp.float32), sketch.T.astype(jnp.float32), precision=lax.Precision.HIGHEST, preferred_element_type=jnp.float32)
    lower_factor = jnp.linalg.cholesky(gram_matrix)
    solved = jax.scipy.linalg.solve_triangular(lower_factor, sketch, lower=True)
    return solved.astype(jnp.bfloat16)

def reference(embeddings, omega, lang_ids):
    first_term = jnp.dot(omega.T.astype(jnp.float32), embeddings.astype(jnp.float32), preferred_element_type=jnp.float32)
    first_basis = orthonormal(first_term)
    scores = jnp.dot(embeddings.astype(jnp.float32), first_basis.T.astype(jnp.float32), preferred_element_type=jnp.float32).astype(jnp.bfloat16)
    second_term = jnp.dot(scores.T.astype(jnp.float32), embeddings.astype(jnp.float32), preferred_element_type=jnp.float32)
    second_basis = orthonormal(second_term)
    coords = jnp.dot(embeddings.astype(jnp.float32), second_basis.T.astype(jnp.float32), preferred_element_type=jnp.float32).astype(jnp.bfloat16)
    devices = N_SK * N_LANG
    per_owner = (LANGS + N_LANG - 1) // N_LANG
    languages = lang_ids[:, 0].reshape(devices, R_DEV)
    member = (languages[:, :, None] == jnp.arange(LANGS, dtype=jnp.int32)[None, None, :]).astype(jnp.int32)
    position = jnp.sum(jnp.cumsum(member, axis=1) * member, axis=2) - 1
    target = languages % N_LANG * (per_owner * CAP) + languages // N_LANG * CAP + position
    source = jnp.broadcast_to(jnp.arange(devices, dtype=jnp.int32)[:, None], (devices, R_DEV))
    outgoing = jnp.zeros((devices, N_LANG * per_owner * CAP, SKETCH), jnp.bfloat16)
    outgoing = outgoing.at[source, target].set(coords.reshape(devices, R_DEV, SKETCH))
    outgoing = outgoing.reshape(N_SK, N_LANG, N_LANG, per_owner * CAP, SKETCH)
    outgoing = jnp.transpose(outgoing, (0, 2, 1, 3, 4))
    return outgoing.reshape(devices * N_LANG * per_owner * CAP, SKETCH)
```

```python
import functools

import jax
import jax.numpy as jnp
from jax import lax
from jax.experimental import pallas as pl
from jax.experimental.pallas import tpu as pltpu
from jax.sharding import PartitionSpec as P

SKETCH = 256
LANGS = 12
CAP = 128
HALF = 128
LANE = 128
F32 = jnp.float32
BF16 = jnp.bfloat16
VMEM = pl.BlockSpec(memory_space=pltpu.VMEM)


def fdot(a, b, ca, cb):
    return lax.dot_general(
        a, b, (((ca,), (cb,)), ((), ())),
        precision=lax.Precision.HIGHEST, preferred_element_type=F32,
    )


def bdot(a, b, ca, cb):
    return lax.dot_general(a, b, (((ca,), (cb,)), ((), ())), preferred_element_type=F32)


def lower_inverse(a):
    lane = lax.broadcasted_iota(jnp.int32, (1, LANE), 1)
    sub = lax.broadcasted_iota(jnp.int32, (8, LANE), 0)
    lane8 = lax.broadcasted_iota(jnp.int32, (8, LANE), 1)
    tiles = [a[8 * i : 8 * i + 8, :] for i in range(HALF // 8)]
    result = []
    for k in range(0, HALF, 4):
        t, s = k // 8, k % 8
        cols = {
            i: [jnp.broadcast_to(tiles[i][:, k + j : k + j + 1], (8, LANE)) for j in range(4)]
            for i in range(t, HALF // 8)
        }
        p = [[cols[t][j][s + i : s + i + 1, :] for j in range(i + 1)] for i in range(4)]
        group = (lane >= k) & (lane < k + 4)
        u, m, inv, root = [], [], [], []
        for i in range(4):
            row = tiles[t][s + i : s + i + 1, :]
            u.append(jnp.where(group, (lane == k + i).astype(F32), row))
        for j in range(4):
            inv.append(1.0 / p[j][j])
            root.append(lax.rsqrt(p[j][j]))
            m.append({i: p[i][j] * inv[j] for i in range(j + 1, 4)})
            for i in range(j + 1, 4):
                for c in range(j + 1, i + 1):
                    p[i][c] = p[i][c] - m[j][i] * p[c][j]
                u[i] = u[i] - m[j][i] * u[j]
        v = [None] * 4
        for j in (3, 2, 1, 0):
            v[j] = u[j] * inv[j]
            for i in range(j + 1, 4):
                v[j] = v[j] - m[j][i] * v[i]
        rows = jnp.zeros((8, LANE), F32)
        for j in range(4):
            rows = jnp.where(sub == s + j, u[j] * root[j], rows)
        rows = jnp.where(lane8 <= sub + 8 * t, rows, 0.0)
        if s == 0:
            result.append(rows)
        else:
            result[t] = result[t] + rows
        for i in range(t if s == 0 else t + 1, HALF // 8):
            tile = jnp.where(group, 0.0, tiles[i])
            low = cols[i][0] * v[0] + cols[i][1] * v[1]
            high = cols[i][2] * v[2] + cols[i][3] * v[3]
            tiles[i] = tile - (low + high)
    return jnp.concatenate(result, axis=0)


def orthonormal_kernel(s_ref, basis_ref):
    sketch = s_ref[...].astype(F32)
    gram = fdot(sketch, sketch, 1, 1)
    first = lower_inverse(gram[:HALF, :HALF])
    across = fdot(gram[HALF:, :HALF], first, 1, 1)
    second = lower_inverse(gram[HALF:, HALF:] - fdot(across, across, 1, 1))
    top = fdot(first, sketch[:HALF], 1, 0)
    basis_ref[:HALF, :] = top.astype(BF16)
    rest = sketch[HALF:] - fdot(across, top, 1, 0)
    basis_ref[HALF:, :] = fdot(second, rest, 1, 0).astype(BF16)


def orthonormal(sketch):
    return pl.pallas_call(
        orthonormal_kernel,
        out_shape=jax.ShapeDtypeStruct(sketch.shape, BF16),
        in_specs=[VMEM],
        out_specs=VMEM,
        compiler_params=pltpu.CompilerParams(vmem_limit_bytes=40 << 20),
        cost_estimate=pl.CostEstimate(flops=2_000_000_000, bytes_accessed=2 << 20, transcendentals=0),
    )(sketch)


def stages_of(sk, lang):
    minor = 2 if sk % 2 == 0 else 1
    return (minor, sk // minor, lang)


def all_sum_kernel(sizes, term_ref, out_ref, acc, *scratch):
    depth = len(sizes)
    send = scratch[0]
    landing = scratch[1 : 1 + depth]
    gathered = scratch[1 + depth]
    send_sems, recv_sems, gsend_sems, grecv_sems = scratch[2 + depth :]
    s, j = lax.axis_index("sk"), lax.axis_index("lang")
    minor = sizes[0]
    mine = (lax.rem(s, minor), s // minor, j)

    def device(stage, index):
        if stage == 0:
            return (s - mine[0] + index, j)
        if stage == 1:
            return (index * minor + mine[0], j)
        return (s, index)

    def peers(stage):
        size = sizes[stage]
        return [(d, lax.rem(mine[stage] + d, size)) for d in range(1, size)]

    barrier = pltpu.get_barrier_semaphore()
    count = 0
    for stage in range(depth):
        for _, index in peers(stage):
            pl.semaphore_signal(
                barrier, inc=1, device_id=device(stage, index), device_id_type=pl.DeviceIdType.MESH
            )
            count += 1

    rows, width = term_ref.shape
    for b in range(width // LANE):
        acc[b * rows : (b + 1) * rows, :] = term_ref[:, b * LANE : (b + 1) * LANE].astype(F32)
    pl.semaphore_wait(barrier, count)

    base, size, slot = 0, acc.shape[0], 0
    spans = []
    for stage in range(depth):
        part = size // sizes[stage]
        copies = []
        for d, index in peers(stage):
            span = pl.ds(pl.multiple_of(base + index * part, part), part)
            send[span, :] = acc[span, :].astype(send.dtype)
            copy = pltpu.make_async_remote_copy(
                src_ref=send.at[span],
                dst_ref=landing[stage].at[d - 1],
                send_sem=send_sems.at[slot + d - 1],
                recv_sem=recv_sems.at[slot + d - 1],
                device_id=device(stage, index),
                device_id_type=pl.DeviceIdType.MESH,
            )
            copy.start()
            copies.append(copy)
        base = base + mine[stage] * part
        own = pl.ds(pl.multiple_of(base, part), part)
        for d, copy in enumerate(copies):
            copy.wait_recv()
        total = acc[own, :]
        for d in range(len(copies)):
            total = total + landing[stage][d].astype(F32)
        acc[own, :] = total
        for copy in copies:
            copy.wait_send()
        spans.append((base, part, slot))
        slot += len(copies)
        size = part

    own = pl.ds(pl.multiple_of(base, size), size)
    gathered[own, :] = acc[own, :].astype(gathered.dtype)
    for stage in reversed(range(depth)):
        base, part, slot = spans[stage]
        span = pl.ds(pl.multiple_of(base, part), part)
        copies = []
        for d, index in peers(stage):
            copy = pltpu.make_async_remote_copy(
                src_ref=gathered.at[span],
                dst_ref=gathered.at[span],
                send_sem=gsend_sems.at[slot + d - 1],
                recv_sem=grecv_sems.at[slot + d - 1],
                device_id=device(stage, index),
                device_id_type=pl.DeviceIdType.MESH,
            )
            copy.start()
            copies.append(copy)
        for copy in copies:
            copy.wait_recv()
        for copy in copies:
            copy.wait_send()
    for b in range(width // LANE):
        out_ref[:, b * LANE : (b + 1) * LANE] = gathered[b * rows : (b + 1) * rows, :]


def all_sum(term, wire, collective_id):
    sizes = stages_of(lax.axis_size("sk"), lax.axis_size("lang"))
    rows, width = term.shape
    flat = rows * width // LANE
    part, landing, slots = flat, [], 0
    for size in sizes:
        part //= size
        landing.append(pltpu.VMEM((max(1, size - 1), max(1, part), LANE), wire))
        slots += size - 1
    if part % 16 or part == 0:
        return lax.psum(term, ("sk", "lang"))
    return pl.pallas_call(
        functools.partial(all_sum_kernel, sizes),
        out_shape=jax.ShapeDtypeStruct((rows, width), wire),
        in_specs=[VMEM],
        out_specs=VMEM,
        scratch_shapes=[
            pltpu.VMEM((flat, LANE), F32),
            pltpu.VMEM((flat, LANE), wire),
            *landing,
            pltpu.VMEM((flat, LANE), wire),
        ]
        + [pltpu.SemaphoreType.DMA((slots,))] * 4,
        compiler_params=pltpu.CompilerParams(
            collective_id=collective_id, has_side_effects=True, vmem_limit_bytes=40 << 20
        ),
    )(term)


def regroup_kernel(lang_count, per_owner, emb_ref, basis_ref, langs_ref, out_ref, target, send, send_sems, recv_sems):
    s, j = lax.axis_index("sk"), lax.axis_index("lang")
    barrier = pltpu.get_barrier_semaphore()
    others = [lax.rem(j + d, lang_count) for d in range(1, lang_count)]
    for index in others:
        pl.semaphore_signal(barrier, inc=1, device_id=(s, index), device_id_type=pl.DeviceIdType.MESH)
    rows = emb_ref.shape[0]
    block = per_owner * CAP
    langs = langs_ref[...]
    padded = -(-LANGS // 16) * 16
    member = lax.broadcasted_iota(jnp.int32, (padded, rows), 0) == langs
    upto = lax.broadcasted_iota(jnp.int32, (rows, rows), 0) <= lax.broadcasted_iota(jnp.int32, (rows, rows), 1)
    earlier = bdot(member.astype(F32).astype(BF16), upto.astype(F32).astype(BF16), 1, 0)
    position = jnp.sum(jnp.where(member, earlier, 0.0), axis=0, keepdims=True).astype(jnp.int32) - 1
    target[...] = lax.rem(langs, lang_count) * block + lax.div(langs, lang_count) * CAP + position
    coords = bdot(emb_ref[...], basis_ref[...], 1, 1).astype(BF16)

    def part(index):
        slots = lax.broadcasted_iota(jnp.int32, (block, rows), 0) + index * block
        chosen = (slots == target[...]).astype(F32).astype(BF16)
        return bdot(chosen, coords, 1, 0).astype(BF16)

    pl.semaphore_wait(barrier, lang_count - 1)
    here = pl.ds(pl.multiple_of(j * block, block), block)
    copies = []
    for d, index in enumerate(others):
        there = pl.ds(d * block, block)
        send[there, :] = part(index)
        copy = pltpu.make_async_remote_copy(
            src_ref=send.at[there],
            dst_ref=out_ref.at[here],
            send_sem=send_sems.at[d],
            recv_sem=recv_sems.at[d],
            device_id=(s, index),
            device_id_type=pl.DeviceIdType.MESH,
        )
        copy.start()
        copies.append(copy)
    out_ref[here, :] = part(j)
    for copy in copies:
        copy.wait()


def regroup(embeddings, basis, lang_ids):
    lang_count = lax.axis_size("lang")
    per_owner = (LANGS + lang_count - 1) // lang_count
    rows = embeddings.shape[0]
    total = lang_count * per_owner * CAP
    return pl.pallas_call(
        functools.partial(regroup_kernel, lang_count, per_owner),
        out_shape=jax.ShapeDtypeStruct((total, SKETCH), BF16),
        in_specs=[VMEM] * 3,
        out_specs=VMEM,
        scratch_shapes=[
            pltpu.VMEM((1, rows), jnp.int32),
            pltpu.VMEM((total, SKETCH), BF16),
            pltpu.SemaphoreType.DMA((lang_count - 1,)),
            pltpu.SemaphoreType.DMA((lang_count - 1,)),
        ],
        compiler_params=pltpu.CompilerParams(
            collective_id=2, has_side_effects=True, vmem_limit_bytes=40 << 20
        ),
    )(embeddings, basis, lang_ids.reshape(1, rows))


WIRE = (F32, F32)


def on_device(embeddings, omega, lang_ids):
    first_term = bdot(omega, embeddings, 0, 0)
    first_basis = orthonormal(all_sum(first_term, WIRE[0], 0))
    scores = bdot(embeddings, first_basis, 1, 1).astype(BF16)
    second_term = bdot(scores, embeddings, 0, 0)
    second_basis = orthonormal(all_sum(second_term, WIRE[1], 1))
    return regroup(embeddings, second_basis, lang_ids)


def solution(mesh):
    spec = P(("sk", "lang"), None)
    return jax.shard_map(
        on_device, mesh=mesh, in_specs=(spec, spec, spec), out_specs=spec, check_vma=False
    )
```

```python
import functools

import jax
import jax.numpy as jnp
from jax import lax
from jax.experimental import pallas as pl
from jax.experimental.pallas import tpu as pltpu
from jax.sharding import PartitionSpec as P

SKETCH = 256
LANGS = 12
CAP = 128
HALF = 128
LANE = 128
F32 = jnp.float32
BF16 = jnp.bfloat16
VMEM = pl.BlockSpec(memory_space=pltpu.VMEM)


def fdot(a, b, ca, cb):
    return lax.dot_general(
        a, b, (((ca,), (cb,)), ((), ())),
        precision=lax.Precision.HIGHEST, preferred_element_type=F32,
    )


def bdot(a, b, ca, cb):
    return lax.dot_general(a, b, (((ca,), (cb,)), ((), ())), preferred_element_type=F32)


def lower_inverse(a, hooks=None):
    lane = lax.broadcasted_iota(jnp.int32, (1, LANE), 1)
    sub = lax.broadcasted_iota(jnp.int32, (8, LANE), 0)
    lane8 = lax.broadcasted_iota(jnp.int32, (8, LANE), 1)
    tiles = [a[8 * i : 8 * i + 8, :] for i in range(HALF // 8)]
    result = []
    for k in range(0, HALF, 4):
        if hooks and k in hooks:
            hooks[k]()
        t, s = k // 8, k % 8
        cols = {
            i: [jnp.broadcast_to(tiles[i][:, k + j : k + j + 1], (8, LANE)) for j in range(4)]
            for i in range(t, HALF // 8)
        }
        p = [[cols[t][j][s + i : s + i + 1, :] for j in range(i + 1)] for i in range(4)]
        group = (lane >= k) & (lane < k + 4)
        u, m, inv, root = [], [], [], []
        for i in range(4):
            row = tiles[t][s + i : s + i + 1, :]
            u.append(jnp.where(group, (lane == k + i).astype(F32), row))
        for j in range(4):
            inv.append(1.0 / p[j][j])
            root.append(lax.rsqrt(p[j][j]))
            m.append({i: p[i][j] * inv[j] for i in range(j + 1, 4)})
            for i in range(j + 1, 4):
                for c in range(j + 1, i + 1):
                    p[i][c] = p[i][c] - m[j][i] * p[c][j]
                u[i] = u[i] - m[j][i] * u[j]
        v = [None] * 4
        for j in (3, 2, 1, 0):
            v[j] = u[j] * inv[j]
            for i in range(j + 1, 4):
                v[j] = v[j] - m[j][i] * v[i]
        rows = jnp.zeros((8, LANE), F32)
        for j in range(4):
            rows = jnp.where(sub == s + j, u[j] * root[j], rows)
        rows = jnp.where(lane8 <= sub + 8 * t, rows, 0.0)
        if s == 0:
            result.append(rows)
        else:
            result[t] = result[t] + rows
        for i in range(t if s == 0 else t + 1, HALF // 8):
            tile = jnp.where(group, 0.0, tiles[i])
            low = cols[i][0] * v[0] + cols[i][1] * v[1]
            high = cols[i][2] * v[2] + cols[i][3] * v[3]
            tiles[i] = tile - (low + high)
    return jnp.concatenate(result, axis=0)


def orthonormal_kernel(s_ref, basis_ref):
    sketch = s_ref[...].astype(F32)
    gram = fdot(sketch, sketch, 1, 1)
    first = lower_inverse(gram[:HALF, :HALF])
    across = fdot(gram[HALF:, :HALF], first, 1, 1)
    second = lower_inverse(gram[HALF:, HALF:] - fdot(across, across, 1, 1))
    top = fdot(first, sketch[:HALF], 1, 0)
    basis_ref[:HALF, :] = top.astype(BF16)
    rest = sketch[HALF:] - fdot(across, top, 1, 0)
    basis_ref[HALF:, :] = fdot(second, rest, 1, 0).astype(BF16)


def orthonormal(sketch):
    return pl.pallas_call(
        orthonormal_kernel,
        out_shape=jax.ShapeDtypeStruct(sketch.shape, BF16),
        in_specs=[VMEM],
        out_specs=VMEM,
        compiler_params=pltpu.CompilerParams(vmem_limit_bytes=40 << 20),
        cost_estimate=pl.CostEstimate(flops=2_000_000_000, bytes_accessed=2 << 20, transcendentals=0),
    )(sketch)


def stages_of(sk, lang):
    minor = 2 if sk % 2 == 0 else 1
    return (minor, sk // minor, lang)


def all_sum_kernel(sizes, term_ref, out_ref, acc, *scratch):
    depth = len(sizes)
    send = scratch[0]
    landing = scratch[1 : 1 + depth]
    gathered = scratch[1 + depth]
    send_sems, recv_sems, gsend_sems, grecv_sems = scratch[2 + depth :]
    s, j = lax.axis_index("sk"), lax.axis_index("lang")
    minor = sizes[0]
    mine = (lax.rem(s, minor), s // minor, j)

    def device(stage, index):
        if stage == 0:
            return (s - mine[0] + index, j)
        if stage == 1:
            return (index * minor + mine[0], j)
        return (s, index)

    def peers(stage):
        size = sizes[stage]
        return [(d, lax.rem(mine[stage] + d, size)) for d in range(1, size)]

    barrier = pltpu.get_barrier_semaphore()
    count = 0
    for stage in range(depth):
        for _, index in peers(stage):
            pl.semaphore_signal(
                barrier, inc=1, device_id=device(stage, index), device_id_type=pl.DeviceIdType.MESH
            )
            count += 1

    rows, width = term_ref.shape
    for b in range(width // LANE):
        acc[b * rows : (b + 1) * rows, :] = term_ref[:, b * LANE : (b + 1) * LANE].astype(F32)
    pl.semaphore_wait(barrier, count)

    base, size, slot = 0, acc.shape[0], 0
    spans = []
    for stage in range(depth):
        part = size // sizes[stage]
        copies = []
        for d, index in peers(stage):
            span = pl.ds(pl.multiple_of(base + index * part, part), part)
            send[span, :] = acc[span, :].astype(send.dtype)
            copy = pltpu.make_async_remote_copy(
                src_ref=send.at[span],
                dst_ref=landing[stage].at[d - 1],
                send_sem=send_sems.at[slot + d - 1],
                recv_sem=recv_sems.at[slot + d - 1],
                device_id=device(stage, index),
                device_id_type=pl.DeviceIdType.MESH,
            )
            copy.start()
            copies.append(copy)
        base = base + mine[stage] * part
        own = pl.ds(pl.multiple_of(base, part), part)
        for d, copy in enumerate(copies):
            copy.wait_recv()
        total = acc[own, :]
        for d in range(len(copies)):
            total = total + landing[stage][d].astype(F32)
        acc[own, :] = total
        for copy in copies:
            copy.wait_send()
        spans.append((base, part, slot))
        slot += len(copies)
        size = part

    own = pl.ds(pl.multiple_of(base, size), size)
    gathered[own, :] = acc[own, :].astype(gathered.dtype)
    for stage in reversed(range(depth)):
        base, part, slot = spans[stage]
        span = pl.ds(pl.multiple_of(base, part), part)
        copies = []
        for d, index in peers(stage):
            copy = pltpu.make_async_remote_copy(
                src_ref=gathered.at[span],
                dst_ref=gathered.at[span],
                send_sem=gsend_sems.at[slot + d - 1],
                recv_sem=grecv_sems.at[slot + d - 1],
                device_id=device(stage, index),
                device_id_type=pl.DeviceIdType.MESH,
            )
            copy.start()
            copies.append(copy)
        for copy in copies:
            copy.wait_recv()
        for copy in copies:
            copy.wait_send()
    for b in range(width // LANE):
        out_ref[:, b * LANE : (b + 1) * LANE] = gathered[b * rows : (b + 1) * rows, :]


def all_sum(term, wire, collective_id):
    sizes = stages_of(lax.axis_size("sk"), lax.axis_size("lang"))
    rows, width = term.shape
    flat = rows * width // LANE
    part, landing, slots = flat, [], 0
    for size in sizes:
        part //= size
        landing.append(pltpu.VMEM((max(1, size - 1), max(1, part), LANE), wire))
        slots += size - 1
    if part % 16 or part == 0:
        return lax.psum(term, ("sk", "lang"))
    return pl.pallas_call(
        functools.partial(all_sum_kernel, sizes),
        out_shape=jax.ShapeDtypeStruct((rows, width), wire),
        in_specs=[VMEM],
        out_specs=VMEM,
        scratch_shapes=[
            pltpu.VMEM((flat, LANE), F32),
            pltpu.VMEM((flat, LANE), wire),
            *landing,
            pltpu.VMEM((flat, LANE), wire),
        ]
        + [pltpu.SemaphoreType.DMA((slots,))] * 4,
        compiler_params=pltpu.CompilerParams(
            collective_id=collective_id, has_side_effects=True, vmem_limit_bytes=40 << 20
        ),
    )(term)


def regroup_kernel(lang_count, per_owner, emb_ref, basis_ref, langs_ref, out_ref, target, send, send_sems, recv_sems):
    s, j = lax.axis_index("sk"), lax.axis_index("lang")
    barrier = pltpu.get_barrier_semaphore()
    others = [lax.rem(j + d, lang_count) for d in range(1, lang_count)]
    for index in others:
        pl.semaphore_signal(barrier, inc=1, device_id=(s, index), device_id_type=pl.DeviceIdType.MESH)
    rows = emb_ref.shape[0]
    block = per_owner * CAP
    langs = langs_ref[...]
    padded = -(-LANGS // 16) * 16
    member = lax.broadcasted_iota(jnp.int32, (padded, rows), 0) == langs
    upto = lax.broadcasted_iota(jnp.int32, (rows, rows), 0) <= lax.broadcasted_iota(jnp.int32, (rows, rows), 1)
    earlier = bdot(member.astype(F32).astype(BF16), upto.astype(F32).astype(BF16), 1, 0)
    position = jnp.sum(jnp.where(member, earlier, 0.0), axis=0, keepdims=True).astype(jnp.int32) - 1
    target[...] = lax.rem(langs, lang_count) * block + lax.div(langs, lang_count) * CAP + position
    coords = bdot(emb_ref[...], basis_ref[...], 1, 1).astype(BF16)

    def part(index):
        slots = lax.broadcasted_iota(jnp.int32, (block, rows), 0) + index * block
        chosen = (slots == target[...]).astype(F32).astype(BF16)
        return bdot(chosen, coords, 1, 0).astype(BF16)

    pl.semaphore_wait(barrier, lang_count - 1)
    here = pl.ds(pl.multiple_of(j * block, block), block)
    copies = []
    for d, index in enumerate(others):
        there = pl.ds(d * block, block)
        send[there, :] = part(index)
        copy = pltpu.make_async_remote_copy(
            src_ref=send.at[there],
            dst_ref=out_ref.at[here],
            send_sem=send_sems.at[d],
            recv_sem=recv_sems.at[d],
            device_id=(s, index),
            device_id_type=pl.DeviceIdType.MESH,
        )
        copy.start()
        copies.append(copy)
    out_ref[here, :] = part(j)
    for copy in copies:
        copy.wait()


def regroup(embeddings, basis, lang_ids):
    lang_count = lax.axis_size("lang")
    per_owner = (LANGS + lang_count - 1) // lang_count
    rows = embeddings.shape[0]
    total = lang_count * per_owner * CAP
    return pl.pallas_call(
        functools.partial(regroup_kernel, lang_count, per_owner),
        out_shape=jax.ShapeDtypeStruct((total, SKETCH), BF16),
        in_specs=[VMEM] * 3,
        out_specs=VMEM,
        scratch_shapes=[
            pltpu.VMEM((1, rows), jnp.int32),
            pltpu.VMEM((total, SKETCH), BF16),
            pltpu.SemaphoreType.DMA((lang_count - 1,)),
            pltpu.SemaphoreType.DMA((lang_count - 1,)),
        ],
        compiler_params=pltpu.CompilerParams(
            collective_id=2, has_side_effects=True, vmem_limit_bytes=40 << 20
        ),
    )(embeddings, basis, lang_ids.reshape(1, rows))


class Piece:
    def __init__(self, sizes, mine, device, acc, landing, gathered, sems):
        self.sizes, self.mine, self.device = sizes, mine, device
        self.acc, self.landing, self.gathered, self.sems = acc, landing, gathered, sems
        self.base, self.size, self.slot = 0, acc.shape[0], 0
        self.spans, self.copies = [], []

    def copy(self, src, dst, slot, stage, index):
        copy = pltpu.make_async_remote_copy(
            src_ref=src,
            dst_ref=dst,
            send_sem=self.sems.at[0, slot],
            recv_sem=self.sems.at[1, slot],
            device_id=self.device(stage, index),
            device_id_type=pl.DeviceIdType.MESH,
        )
        copy.start()
        self.copies.append(copy)

    def send(self, stage):
        size = self.sizes[stage]
        part = self.size // size
        for d in range(1, size):
            index = lax.rem(self.mine[stage] + d, size)
            span = pl.ds(pl.multiple_of(self.base + index * part, part), part)
            self.copy(self.acc.at[span], self.landing[stage].at[d - 1], self.slot + d - 1, stage, index)

    def add(self, stage):
        size = self.sizes[stage]
        part = self.size // size
        base = self.base + self.mine[stage] * part
        own = pl.ds(pl.multiple_of(base, part), part)
        for copy in self.copies:
            copy.wait_recv()
        total = self.acc[own, :]
        for d in range(1, size):
            total = total + self.landing[stage][d - 1]
        last = stage == len(self.sizes) - 1
        (self.gathered if last else self.acc)[own, :] = total
        for copy in self.copies:
            copy.wait_send()
        self.copies = []
        self.base, self.size, self.slot = base, part, self.slot + size - 1
        self.spans.append((base, part))

    def spread(self, stage):
        base, part = self.spans[stage]
        span = pl.ds(pl.multiple_of(base, part), part)
        for d in range(1, self.sizes[stage]):
            index = lax.rem(self.mine[stage] + d, self.sizes[stage])
            self.copy(self.gathered.at[span], self.gathered.at[span], self.slot + d - 1, stage, index)
        self.slot += self.sizes[stage] - 1

    def land(self):
        for copy in self.copies:
            copy.wait_recv()
        for copy in self.copies:
            copy.wait_send()
        self.copies = []

    def put(self, term):
        for b in range(term.shape[1] // LANE):
            self.acc[b * HALF : (b + 1) * HALF, :] = term[:, b * LANE : (b + 1) * LANE]

    def get(self):
        blocks = self.gathered.shape[0] // HALF
        return jnp.concatenate([self.gathered[b * HALF : (b + 1) * HALF, :] for b in range(blocks)], axis=1)


def whole_kernel(sizes, per_owner, emb_ref, omega_ref, langs_ref, out_ref, *scratch):
    minor, lang_count = sizes[0], sizes[2]
    s, j = lax.axis_index("sk"), lax.axis_index("lang")
    mine = (lax.rem(s, minor), s // minor, j)
    chosen, outgoing, out_sems = scratch[:3]

    def device(stage, index):
        if stage == 0:
            return (s - mine[0] + index, j)
        if stage == 1:
            return (index * minor + mine[0], j)
        return (s, index)

    pieces = []
    for n in range(4):
        part = scratch[3 + 6 * n : 9 + 6 * n]
        pieces.append(Piece(sizes, mine, device, part[0], part[1:4], part[4], part[5]))
    a1, b1, a2, b2 = pieces

    barrier = pltpu.get_barrier_semaphore()
    count = 0
    for stage in range(3):
        for d in range(1, sizes[stage]):
            pl.semaphore_signal(
                barrier,
                inc=1,
                device_id=device(stage, lax.rem(mine[stage] + d, sizes[stage])),
                device_id_type=pl.DeviceIdType.MESH,
            )
            count += 1

    block = per_owner * CAP
    rows = emb_ref.shape[0]
    others = [lax.rem(j + d, lang_count) for d in range(1, lang_count)]

    def choose():
        langs = langs_ref[...]
        padded = -(-LANGS // 16) * 16
        member = lax.broadcasted_iota(jnp.int32, (padded, rows), 0) == langs
        upto = lax.broadcasted_iota(jnp.int32, (rows, rows), 0) <= lax.broadcasted_iota(jnp.int32, (rows, rows), 1)
        earlier = bdot(member.astype(F32).astype(BF16), upto.astype(F32).astype(BF16), 1, 0)
        position = jnp.sum(jnp.where(member, earlier, 0.0), axis=0, keepdims=True).astype(jnp.int32) - 1
        target = lax.rem(langs, lang_count) * block + lax.div(langs, lang_count) * CAP + position
        slots = lax.broadcasted_iota(jnp.int32, (block, rows), 0)
        for n, index in enumerate(others + [j]):
            chosen[n * block : (n + 1) * block, :] = (slots + index * block == target).astype(F32).astype(BF16)

    def power(piece, basis):
        scores = bdot(basis, emb_ref[...], 1, 1).astype(BF16)
        piece.put(bdot(scores, emb_ref[...], 1, 0))

    def hand_out(basis, half):
        coords = bdot(emb_ref[...], basis, 1, 1).astype(BF16)
        here = pl.ds(pl.multiple_of(j * block, block), block)
        lanes = pl.ds(half * HALF, HALF)
        copies = []
        for n, index in enumerate(others):
            span = pl.ds(n * block, block)
            outgoing[half, span, :] = bdot(chosen[span, :], coords, 1, 0).astype(BF16)
            copy = pltpu.make_async_remote_copy(
                src_ref=outgoing.at[half, span],
                dst_ref=out_ref.at[here, lanes],
                send_sem=out_sems.at[0, half, n],
                recv_sem=out_sems.at[1, half, n],
                device_id=(s, index),
                device_id_type=pl.DeviceIdType.MESH,
            )
            copy.start()
            copies.append(copy)
        own = chosen[len(others) * block : (len(others) + 1) * block, :]
        out_ref[here, half * HALF : (half + 1) * HALF] = bdot(own, coords, 1, 0).astype(BF16)
        return copies

    a1.put(bdot(omega_ref[:, :HALF], emb_ref[...], 0, 0))
    pl.semaphore_wait(barrier, count)
    a1.send(0)
    b1.put(bdot(omega_ref[:, HALF:], emb_ref[...], 0, 0))
    b1.send(0)
    a1.add(0)
    a1.send(1)
    b1.add(0)
    b1.send(1)
    choose()
    a1.add(1)
    a1.send(2)
    b1.add(1)
    b1.send(2)
    a1.add(2)
    a1.spread(2)
    b1.add(2)
    b1.spread(2)
    a1.land()
    a1.spread(1)
    b1.land()
    a1.land()
    a1.spread(0)
    b1.spread(1)
    a1.land()

    def b1_last():
        b1.land()
        b1.spread(0)

    first = a1.get()
    inverse = lower_inverse(fdot(first, first, 1, 1), {96: b1_last})
    top = fdot(inverse, first, 1, 0)
    power(a2, top.astype(BF16))
    a2.send(0)
    b1.land()

    second = b1.get()
    across = fdot(fdot(second, first, 1, 1), inverse, 1, 1)
    corner = fdot(second, second, 1, 1) - fdot(across, across, 1, 1)
    a2.add(0)
    a2.send(1)
    rest = second - fdot(across, top, 1, 0)
    inverse = lower_inverse(corner)
    a2.add(1)
    a2.send(2)
    power(b2, fdot(inverse, rest, 1, 0).astype(BF16))
    b2.send(0)
    a2.add(2)
    a2.spread(2)
    b2.add(0)
    b2.send(1)
    a2.land()
    a2.spread(1)
    b2.add(1)
    b2.send(2)
    a2.land()
    a2.spread(0)
    b2.add(2)
    b2.spread(2)
    a2.land()

    def b2_middle():
        b2.land()
        b2.spread(1)

    def b2_last():
        b2.land()
        b2.spread(0)

    first = a2.get()
    inverse = lower_inverse(fdot(first, first, 1, 1), {32: b2_middle, 120: b2_last})
    top = fdot(inverse, first, 1, 0)
    copies = hand_out(top.astype(BF16), 0)
    b2.land()
    second = b2.get()
    across = fdot(fdot(second, first, 1, 1), inverse, 1, 1)
    corner = fdot(second, second, 1, 1) - fdot(across, across, 1, 1)
    rest = second - fdot(across, top, 1, 0)
    inverse = lower_inverse(corner)
    copies += hand_out(fdot(inverse, rest, 1, 0).astype(BF16), 1)
    for copy in copies:
        copy.wait()


def in_one_kernel(sizes, embeddings, omega, lang_ids):
    rows, width = embeddings.shape
    lang_count = sizes[2]
    per_owner = (LANGS + lang_count - 1) // lang_count
    total = lang_count * per_owner * CAP
    flat = HALF * width // LANE
    slots = 2 * sum(size - 1 for size in sizes)
    part, landing = flat, []
    for size in sizes:
        part //= size
        landing.append(pltpu.VMEM((max(1, size - 1), part, LANE), F32))
    piece = [
        pltpu.VMEM((flat, LANE), F32),
        *landing,
        pltpu.VMEM((flat, LANE), F32),
        pltpu.SemaphoreType.DMA((2, slots)),
    ]
    return pl.pallas_call(
        functools.partial(whole_kernel, sizes, per_owner),
        out_shape=jax.ShapeDtypeStruct((total, SKETCH), BF16),
        in_specs=[VMEM] * 3,
        out_specs=VMEM,
        scratch_shapes=[
            pltpu.VMEM((total, rows), BF16),
            pltpu.VMEM((2, (lang_count - 1) * per_owner * CAP, HALF), BF16),
            pltpu.SemaphoreType.DMA((2, 2, lang_count - 1)),
            *(piece * 4),
        ],
        compiler_params=pltpu.CompilerParams(
            collective_id=3, has_side_effects=True, vmem_limit_bytes=48 << 20
        ),
    )(embeddings, omega, lang_ids.reshape(1, rows))


WIRE = (F32, F32)


def on_device(embeddings, omega, lang_ids):
    sizes = stages_of(lax.axis_size("sk"), lax.axis_size("lang"))
    flat = HALF * embeddings.shape[1] // LANE
    if flat % (8 * sizes[0] * sizes[1] * sizes[2]) == 0:
        return in_one_kernel(sizes, embeddings, omega, lang_ids)
    first_term = bdot(omega, embeddings, 0, 0)
    first_basis = orthonormal(all_sum(first_term, WIRE[0], 0))
    scores = bdot(embeddings, first_basis, 1, 1).astype(BF16)
    second_term = bdot(scores, embeddings, 0, 0)
    second_basis = orthonormal(all_sum(second_term, WIRE[1], 1))
    return regroup(embeddings, second_basis, lang_ids)


def solution(mesh):
    spec = P(("sk", "lang"), None)
    return jax.shard_map(
        on_device, mesh=mesh, in_specs=(spec, spec, spec), out_specs=spec, check_vma=False
    )
```

```python
import functools

import jax
import jax.numpy as jnp
from jax import lax
from jax.experimental import pallas as pl
from jax.experimental.pallas import tpu as pltpu
from jax.sharding import PartitionSpec as P

SKETCH = 256
LANGS = 12
CAP = 128
HALF = 128
LANE = 128
F32 = jnp.float32
BF16 = jnp.bfloat16
VMEM = pl.BlockSpec(memory_space=pltpu.VMEM)


def fdot(a, b, ca, cb):
    return lax.dot_general(
        a, b, (((ca,), (cb,)), ((), ())),
        precision=lax.Precision.HIGHEST, preferred_element_type=F32,
    )


def bdot(a, b, ca, cb):
    return lax.dot_general(a, b, (((ca,), (cb,)), ((), ())), preferred_element_type=F32)


def lower_inverse(a, hooks=None):
    lane = lax.broadcasted_iota(jnp.int32, (1, LANE), 1)
    sub = lax.broadcasted_iota(jnp.int32, (8, LANE), 0)
    lane8 = lax.broadcasted_iota(jnp.int32, (8, LANE), 1)
    tiles = [a[8 * i : 8 * i + 8, :] for i in range(HALF // 8)]
    result = []
    for k in range(0, HALF, 4):
        if hooks and k in hooks:
            hooks[k]()
        t, s = k // 8, k % 8
        cols = {
            i: [jnp.broadcast_to(tiles[i][:, k + j : k + j + 1], (8, LANE)) for j in range(4)]
            for i in range(t, HALF // 8)
        }
        p = [[cols[t][j][s + i : s + i + 1, :] for j in range(i + 1)] for i in range(4)]
        group = (lane >= k) & (lane < k + 4)
        u, m, inv, root = [], [], [], []
        for i in range(4):
            row = tiles[t][s + i : s + i + 1, :]
            u.append(jnp.where(group, (lane == k + i).astype(F32), row))
        for j in range(4):
            inv.append(1.0 / p[j][j])
            root.append(lax.rsqrt(p[j][j]))
            m.append({i: p[i][j] * inv[j] for i in range(j + 1, 4)})
            for i in range(j + 1, 4):
                for c in range(j + 1, i + 1):
                    p[i][c] = p[i][c] - m[j][i] * p[c][j]
                u[i] = u[i] - m[j][i] * u[j]
        v = [None] * 4
        for j in (3, 2, 1, 0):
            v[j] = u[j] * inv[j]
            for i in range(j + 1, 4):
                v[j] = v[j] - m[j][i] * v[i]
        rows = jnp.zeros((8, LANE), F32)
        for j in range(4):
            rows = jnp.where(sub == s + j, u[j] * root[j], rows)
        rows = jnp.where(lane8 <= sub + 8 * t, rows, 0.0)
        if s == 0:
            result.append(rows)
        else:
            result[t] = result[t] + rows
        for i in range(t if s == 0 else t + 1, HALF // 8):
            tile = jnp.where(group, 0.0, tiles[i])
            low = cols[i][0] * v[0] + cols[i][1] * v[1]
            high = cols[i][2] * v[2] + cols[i][3] * v[3]
            tiles[i] = tile - (low + high)
    return jnp.concatenate(result, axis=0)


def orthonormal_kernel(s_ref, basis_ref):
    sketch = s_ref[...].astype(F32)
    gram = fdot(sketch, sketch, 1, 1)
    first = lower_inverse(gram[:HALF, :HALF])
    across = fdot(gram[HALF:, :HALF], first, 1, 1)
    second = lower_inverse(gram[HALF:, HALF:] - fdot(across, across, 1, 1))
    top = fdot(first, sketch[:HALF], 1, 0)
    basis_ref[:HALF, :] = top.astype(BF16)
    rest = sketch[HALF:] - fdot(across, top, 1, 0)
    basis_ref[HALF:, :] = fdot(second, rest, 1, 0).astype(BF16)


def orthonormal(sketch):
    return pl.pallas_call(
        orthonormal_kernel,
        out_shape=jax.ShapeDtypeStruct(sketch.shape, BF16),
        in_specs=[VMEM],
        out_specs=VMEM,
        compiler_params=pltpu.CompilerParams(vmem_limit_bytes=40 << 20),
        cost_estimate=pl.CostEstimate(flops=2_000_000_000, bytes_accessed=2 << 20, transcendentals=0),
    )(sketch)


def stages_of(sk, lang):
    minor = 2 if sk % 2 == 0 else 1
    return (minor, sk // minor, lang)


def all_sum_kernel(sizes, term_ref, out_ref, acc, *scratch):
    depth = len(sizes)
    send = scratch[0]
    landing = scratch[1 : 1 + depth]
    gathered = scratch[1 + depth]
    send_sems, recv_sems, gsend_sems, grecv_sems = scratch[2 + depth :]
    s, j = lax.axis_index("sk"), lax.axis_index("lang")
    minor = sizes[0]
    mine = (lax.rem(s, minor), s // minor, j)

    def device(stage, index):
        if stage == 0:
            return (s - mine[0] + index, j)
        if stage == 1:
            return (index * minor + mine[0], j)
        return (s, index)

    def peers(stage):
        size = sizes[stage]
        return [(d, lax.rem(mine[stage] + d, size)) for d in range(1, size)]

    barrier = pltpu.get_barrier_semaphore()
    count = 0
    for stage in range(depth):
        for _, index in peers(stage):
            pl.semaphore_signal(
                barrier, inc=1, device_id=device(stage, index), device_id_type=pl.DeviceIdType.MESH
            )
            count += 1

    rows, width = term_ref.shape
    for b in range(width // LANE):
        acc[b * rows : (b + 1) * rows, :] = term_ref[:, b * LANE : (b + 1) * LANE].astype(F32)
    pl.semaphore_wait(barrier, count)

    base, size, slot = 0, acc.shape[0], 0
    spans = []
    for stage in range(depth):
        part = size // sizes[stage]
        copies = []
        for d, index in peers(stage):
            span = pl.ds(pl.multiple_of(base + index * part, part), part)
            send[span, :] = acc[span, :].astype(send.dtype)
            copy = pltpu.make_async_remote_copy(
                src_ref=send.at[span],
                dst_ref=landing[stage].at[d - 1],
                send_sem=send_sems.at[slot + d - 1],
                recv_sem=recv_sems.at[slot + d - 1],
                device_id=device(stage, index),
                device_id_type=pl.DeviceIdType.MESH,
            )
            copy.start()
            copies.append(copy)
        base = base + mine[stage] * part
        own = pl.ds(pl.multiple_of(base, part), part)
        for d, copy in enumerate(copies):
            copy.wait_recv()
        total = acc[own, :]
        for d in range(len(copies)):
            total = total + landing[stage][d].astype(F32)
        acc[own, :] = total
        for copy in copies:
            copy.wait_send()
        spans.append((base, part, slot))
        slot += len(copies)
        size = part

    own = pl.ds(pl.multiple_of(base, size), size)
    gathered[own, :] = acc[own, :].astype(gathered.dtype)
    for stage in reversed(range(depth)):
        base, part, slot = spans[stage]
        span = pl.ds(pl.multiple_of(base, part), part)
        copies = []
        for d, index in peers(stage):
            copy = pltpu.make_async_remote_copy(
                src_ref=gathered.at[span],
                dst_ref=gathered.at[span],
                send_sem=gsend_sems.at[slot + d - 1],
                recv_sem=grecv_sems.at[slot + d - 1],
                device_id=device(stage, index),
                device_id_type=pl.DeviceIdType.MESH,
            )
            copy.start()
            copies.append(copy)
        for copy in copies:
            copy.wait_recv()
        for copy in copies:
            copy.wait_send()
    for b in range(width // LANE):
        out_ref[:, b * LANE : (b + 1) * LANE] = gathered[b * rows : (b + 1) * rows, :]


def all_sum(term, wire, collective_id):
    sizes = stages_of(lax.axis_size("sk"), lax.axis_size("lang"))
    rows, width = term.shape
    flat = rows * width // LANE
    part, landing, slots = flat, [], 0
    for size in sizes:
        part //= size
        landing.append(pltpu.VMEM((max(1, size - 1), max(1, part), LANE), wire))
        slots += size - 1
    if part % 16 or part == 0:
        return lax.psum(term, ("sk", "lang"))
    return pl.pallas_call(
        functools.partial(all_sum_kernel, sizes),
        out_shape=jax.ShapeDtypeStruct((rows, width), wire),
        in_specs=[VMEM],
        out_specs=VMEM,
        scratch_shapes=[
            pltpu.VMEM((flat, LANE), F32),
            pltpu.VMEM((flat, LANE), wire),
            *landing,
            pltpu.VMEM((flat, LANE), wire),
        ]
        + [pltpu.SemaphoreType.DMA((slots,))] * 4,
        compiler_params=pltpu.CompilerParams(
            collective_id=collective_id, has_side_effects=True, vmem_limit_bytes=40 << 20
        ),
    )(term)


def regroup_kernel(lang_count, per_owner, emb_ref, basis_ref, langs_ref, out_ref, target, send, send_sems, recv_sems):
    s, j = lax.axis_index("sk"), lax.axis_index("lang")
    barrier = pltpu.get_barrier_semaphore()
    others = [lax.rem(j + d, lang_count) for d in range(1, lang_count)]
    for index in others:
        pl.semaphore_signal(barrier, inc=1, device_id=(s, index), device_id_type=pl.DeviceIdType.MESH)
    rows = emb_ref.shape[0]
    block = per_owner * CAP
    langs = langs_ref[...]
    padded = -(-LANGS // 16) * 16
    member = lax.broadcasted_iota(jnp.int32, (padded, rows), 0) == langs
    upto = lax.broadcasted_iota(jnp.int32, (rows, rows), 0) <= lax.broadcasted_iota(jnp.int32, (rows, rows), 1)
    earlier = bdot(member.astype(F32).astype(BF16), upto.astype(F32).astype(BF16), 1, 0)
    position = jnp.sum(jnp.where(member, earlier, 0.0), axis=0, keepdims=True).astype(jnp.int32) - 1
    target[...] = lax.rem(langs, lang_count) * block + lax.div(langs, lang_count) * CAP + position
    coords = bdot(emb_ref[...], basis_ref[...], 1, 1).astype(BF16)

    def part(index):
        slots = lax.broadcasted_iota(jnp.int32, (block, rows), 0) + index * block
        chosen = (slots == target[...]).astype(F32).astype(BF16)
        return bdot(chosen, coords, 1, 0).astype(BF16)

    pl.semaphore_wait(barrier, lang_count - 1)
    here = pl.ds(pl.multiple_of(j * block, block), block)
    copies = []
    for d, index in enumerate(others):
        there = pl.ds(d * block, block)
        send[there, :] = part(index)
        copy = pltpu.make_async_remote_copy(
            src_ref=send.at[there],
            dst_ref=out_ref.at[here],
            send_sem=send_sems.at[d],
            recv_sem=recv_sems.at[d],
            device_id=(s, index),
            device_id_type=pl.DeviceIdType.MESH,
        )
        copy.start()
        copies.append(copy)
    out_ref[here, :] = part(j)
    for copy in copies:
        copy.wait()


def regroup(embeddings, basis, lang_ids):
    lang_count = lax.axis_size("lang")
    per_owner = (LANGS + lang_count - 1) // lang_count
    rows = embeddings.shape[0]
    total = lang_count * per_owner * CAP
    return pl.pallas_call(
        functools.partial(regroup_kernel, lang_count, per_owner),
        out_shape=jax.ShapeDtypeStruct((total, SKETCH), BF16),
        in_specs=[VMEM] * 3,
        out_specs=VMEM,
        scratch_shapes=[
            pltpu.VMEM((1, rows), jnp.int32),
            pltpu.VMEM((total, SKETCH), BF16),
            pltpu.SemaphoreType.DMA((lang_count - 1,)),
            pltpu.SemaphoreType.DMA((lang_count - 1,)),
        ],
        compiler_params=pltpu.CompilerParams(
            collective_id=2, has_side_effects=True, vmem_limit_bytes=40 << 20
        ),
    )(embeddings, basis, lang_ids.reshape(1, rows))


class Piece:
    def __init__(self, sizes, mine, device, acc, landing, gathered, sems):
        self.sizes, self.mine, self.device = sizes, mine, device
        self.acc, self.landing, self.gathered, self.sems = acc, landing, gathered, sems
        self.base, self.size, self.slot = 0, acc.shape[0], 0
        self.spans, self.copies = [], []

    def copy(self, src, dst, slot, stage, index):
        copy = pltpu.make_async_remote_copy(
            src_ref=src,
            dst_ref=dst,
            send_sem=self.sems.at[0, slot],
            recv_sem=self.sems.at[1, slot],
            device_id=self.device(stage, index),
            device_id_type=pl.DeviceIdType.MESH,
        )
        copy.start()
        self.copies.append(copy)

    def send(self, stage):
        size = self.sizes[stage]
        part = self.size // size
        for d in range(1, size):
            index = lax.rem(self.mine[stage] + d, size)
            span = pl.ds(pl.multiple_of(self.base + index * part, part), part)
            self.copy(self.acc.at[span], self.landing[stage].at[d - 1], self.slot + d - 1, stage, index)

    def add(self, stage):
        size = self.sizes[stage]
        part = self.size // size
        base = self.base + self.mine[stage] * part
        own = pl.ds(pl.multiple_of(base, part), part)
        for copy in self.copies:
            copy.wait_recv()
        total = self.acc[own, :]
        for d in range(1, size):
            total = total + self.landing[stage][d - 1]
        last = stage == len(self.sizes) - 1
        (self.gathered if last else self.acc)[own, :] = total
        for copy in self.copies:
            copy.wait_send()
        self.copies = []
        self.base, self.size, self.slot = base, part, self.slot + size - 1
        self.spans.append((base, part))

    def spread(self, stage):
        base, part = self.spans[stage]
        span = pl.ds(pl.multiple_of(base, part), part)
        for d in range(1, self.sizes[stage]):
            index = lax.rem(self.mine[stage] + d, self.sizes[stage])
            self.copy(self.gathered.at[span], self.gathered.at[span], self.slot + d - 1, stage, index)
        self.slot += self.sizes[stage] - 1

    def land(self):
        for copy in self.copies:
            copy.wait_recv()
        for copy in self.copies:
            copy.wait_send()
        self.copies = []

    def put(self, term):
        for b in range(term.shape[1] // LANE):
            self.acc[b * HALF : (b + 1) * HALF, :] = term[:, b * LANE : (b + 1) * LANE]

    def get(self):
        blocks = self.gathered.shape[0] // HALF
        return jnp.concatenate([self.gathered[b * HALF : (b + 1) * HALF, :] for b in range(blocks)], axis=1)


def whole_kernel(sizes, per_owner, emb_ref, term_ref, langs_ref, out_ref, *scratch):
    minor, lang_count = sizes[0], sizes[2]
    s, j = lax.axis_index("sk"), lax.axis_index("lang")
    mine = (lax.rem(s, minor), s // minor, j)
    chosen, outgoing, out_sems = scratch[:3]

    def device(stage, index):
        if stage == 0:
            return (s - mine[0] + index, j)
        if stage == 1:
            return (index * minor + mine[0], j)
        return (s, index)

    pieces = []
    for n in range(4):
        part = scratch[3 + 6 * n : 9 + 6 * n]
        pieces.append(Piece(sizes, mine, device, part[0], part[1:4], part[4], part[5]))
    a1, b1, a2, b2 = pieces

    barrier = pltpu.get_barrier_semaphore()
    count = 0
    for stage in range(3):
        for d in range(1, sizes[stage]):
            pl.semaphore_signal(
                barrier,
                inc=1,
                device_id=device(stage, lax.rem(mine[stage] + d, sizes[stage])),
                device_id_type=pl.DeviceIdType.MESH,
            )
            count += 1

    block = per_owner * CAP
    rows = emb_ref.shape[0]
    others = [lax.rem(j + d, lang_count) for d in range(1, lang_count)]

    def choose():
        langs = langs_ref[...]
        padded = -(-LANGS // 16) * 16
        member = lax.broadcasted_iota(jnp.int32, (padded, rows), 0) == langs
        upto = lax.broadcasted_iota(jnp.int32, (rows, rows), 0) <= lax.broadcasted_iota(jnp.int32, (rows, rows), 1)
        earlier = bdot(member.astype(F32).astype(BF16), upto.astype(F32).astype(BF16), 1, 0)
        position = jnp.sum(jnp.where(member, earlier, 0.0), axis=0, keepdims=True).astype(jnp.int32) - 1
        target = lax.rem(langs, lang_count) * block + lax.div(langs, lang_count) * CAP + position
        slots = lax.broadcasted_iota(jnp.int32, (block, rows), 0)
        for n, index in enumerate(others + [j]):
            chosen[n * block : (n + 1) * block, :] = (slots + index * block == target).astype(F32).astype(BF16)

    def power(piece, basis):
        scores = bdot(basis, emb_ref[...], 1, 1).astype(BF16)
        piece.put(bdot(scores, emb_ref[...], 1, 0))

    def hand_out(basis, half):
        coords = bdot(emb_ref[...], basis, 1, 1).astype(BF16)
        here = pl.ds(pl.multiple_of(j * block, block), block)
        lanes = pl.ds(half * HALF, HALF)
        copies = []
        for n, index in enumerate(others):
            span = pl.ds(n * block, block)
            outgoing[half, span, :] = bdot(chosen[span, :], coords, 1, 0).astype(BF16)
            copy = pltpu.make_async_remote_copy(
                src_ref=outgoing.at[half, span],
                dst_ref=out_ref.at[here, lanes],
                send_sem=out_sems.at[0, half, n],
                recv_sem=out_sems.at[1, half, n],
                device_id=(s, index),
                device_id_type=pl.DeviceIdType.MESH,
            )
            copy.start()
            copies.append(copy)
        own = chosen[len(others) * block : (len(others) + 1) * block, :]
        out_ref[here, half * HALF : (half + 1) * HALF] = bdot(own, coords, 1, 0).astype(BF16)
        return copies

    a1.put(term_ref[:HALF, :])
    pl.semaphore_wait(barrier, count)
    a1.send(0)
    b1.put(term_ref[HALF:, :])
    b1.send(0)
    a1.add(0)
    a1.send(1)
    b1.add(0)
    b1.send(1)
    choose()
    a1.add(1)
    a1.send(2)
    b1.add(1)
    b1.send(2)
    a1.add(2)
    a1.spread(2)
    b1.add(2)
    b1.spread(2)
    a1.land()
    a1.spread(1)
    b1.land()
    a1.land()
    a1.spread(0)
    b1.spread(1)
    a1.land()

    def b1_last():
        b1.land()
        b1.spread(0)

    first = a1.get()
    inverse = lower_inverse(fdot(first, first, 1, 1), {96: b1_last})
    top = fdot(inverse, first, 1, 0)
    power(a2, top.astype(BF16))
    a2.send(0)
    b1.land()

    second = b1.get()
    across = fdot(fdot(second, first, 1, 1), inverse, 1, 1)
    corner = fdot(second, second, 1, 1) - fdot(across, across, 1, 1)
    a2.add(0)
    a2.send(1)
    rest = second - fdot(across, top, 1, 0)
    inverse = lower_inverse(corner)
    a2.add(1)
    a2.send(2)
    power(b2, fdot(inverse, rest, 1, 0).astype(BF16))
    b2.send(0)
    a2.add(2)
    a2.spread(2)
    b2.add(0)
    b2.send(1)
    a2.land()
    a2.spread(1)
    b2.add(1)
    b2.send(2)
    a2.land()
    a2.spread(0)
    b2.add(2)
    b2.spread(2)
    a2.land()

    def b2_middle():
        b2.land()
        b2.spread(1)

    def b2_last():
        b2.land()
        b2.spread(0)

    first = a2.get()
    inverse = lower_inverse(fdot(first, first, 1, 1), {32: b2_middle, 120: b2_last})
    top = fdot(inverse, first, 1, 0)
    copies = hand_out(top.astype(BF16), 0)
    b2.land()
    second = b2.get()
    across = fdot(fdot(second, first, 1, 1), inverse, 1, 1)
    corner = fdot(second, second, 1, 1) - fdot(across, across, 1, 1)
    rest = second - fdot(across, top, 1, 0)
    inverse = lower_inverse(corner)
    copies += hand_out(fdot(inverse, rest, 1, 0).astype(BF16), 1)
    for copy in copies:
        copy.wait()


def in_one_kernel(sizes, embeddings, term, lang_ids):
    rows, width = embeddings.shape
    lang_count = sizes[2]
    per_owner = (LANGS + lang_count - 1) // lang_count
    total = lang_count * per_owner * CAP
    flat = HALF * width // LANE
    slots = 2 * sum(size - 1 for size in sizes)
    part, landing = flat, []
    for size in sizes:
        part //= size
        landing.append(pltpu.VMEM((max(1, size - 1), part, LANE), F32))
    piece = [
        pltpu.VMEM((flat, LANE), F32),
        *landing,
        pltpu.VMEM((flat, LANE), F32),
        pltpu.SemaphoreType.DMA((2, slots)),
    ]
    return pl.pallas_call(
        functools.partial(whole_kernel, sizes, per_owner),
        out_shape=jax.ShapeDtypeStruct((total, SKETCH), BF16),
        in_specs=[VMEM] * 3,
        out_specs=VMEM,
        scratch_shapes=[
            pltpu.VMEM((total, rows), BF16),
            pltpu.VMEM((2, (lang_count - 1) * per_owner * CAP, HALF), BF16),
            pltpu.SemaphoreType.DMA((2, 2, lang_count - 1)),
            *(piece * 4),
        ],
        compiler_params=pltpu.CompilerParams(
            collective_id=3, has_side_effects=True, vmem_limit_bytes=48 << 20
        ),
    )(embeddings, term, lang_ids.reshape(1, rows))


WIRE = (F32, F32)


def on_device(embeddings, omega, lang_ids):
    first_term = bdot(omega, embeddings, 0, 0)
    sizes = stages_of(lax.axis_size("sk"), lax.axis_size("lang"))
    flat = HALF * embeddings.shape[1] // LANE
    if flat % (8 * sizes[0] * sizes[1] * sizes[2]) == 0:
        return in_one_kernel(sizes, embeddings, first_term, lang_ids)
    first_basis = orthonormal(all_sum(first_term, WIRE[0], 0))
    scores = bdot(embeddings, first_basis, 1, 1).astype(BF16)
    second_term = bdot(scores, embeddings, 0, 0)
    second_basis = orthonormal(all_sum(second_term, WIRE[1], 1))
    return regroup(embeddings, second_basis, lang_ids)


def solution(mesh):
    spec = P(("sk", "lang"), None)
    return jax.shard_map(
        on_device, mesh=mesh, in_specs=(spec, spec, spec), out_specs=spec, check_vma=False
    )
```
